32 devices in a mesh: plane: 4 (over z), pencil: 8 (over y, x, core).
Axes of the slice: x: 2, y: 2, z: 4, core: 2. Of those that a mesh axis runs over, the one named last changes fastest.
Arguments:
- velocity: float32 [8, 5120, 3840], P('plane', 'pencil'), may hold values from -6 to 6
- plane_slot: int32 [8], replicated, may hold values from 0 to 7, as said below
- pair_list: int32 [20, 2], replicated, may hold values from 0 to 7, as said below
Outputs:
- band_cross: float32 [8, 4, 2, 1024, 512], P('plane', None, None, 'pencil')
- partner_cross: float32 [8, 4, 2, 1024, 512], P('plane', None, None, 'pencil')
The draws below stay inside these ranges and needn't reach their ends.
Inputs may be any that keep to these rules, and one draw needn't show every extreme that they name: Plane q is held in slot plane_slot[q] of velocity; that slot lies in the same aligned block of 2 slots as q, and every slot holds exactly one plane. `pair_list`: each row (a, b) satisfies a <= b < a + 4; no row appears twice; rows (0, 0) and (7, 7) are present.
All inputs are finite; a program needn't handle non-finite values.
Results may differ from the reference program's by a relative error of at most 0.000088.
Values sent between devices are 32-bit elements; how exact they have to be, the bound alone decides.
No kernel may reach another device: no remote copies, remote signals or barrier semaphores. Data moves between devices by JAX's collectives and lax.ppermute only.
A program may use at most 128 MiB of HBM per device.

```python
import math
import jax
import jax.numpy as jnp
from jax import lax

NX = 5120
NZ = 3840
KX = 512
KZ = 1024
PL_DEV = 2
PLANES = 8
BAND = 4
PAIRS = 20


def draw_plane_slot(key, part):
    blocks = PLANES // PL_DEV
    scores = jax.random.randint(key, (blocks, PL_DEV), 0, 1048576) * PL_DEV + lax.broadcasted_iota(jnp.int32, (blocks, PL_DEV), 1)
    ordering = jnp.argsort(scores, axis=1, stable=True).astype(jnp.int32)
    block_start = lax.broadcasted_iota(jnp.int32, (blocks, PL_DEV), 0) * PL_DEV
    return (block_start + ordering).reshape(PLANES).astype(jnp.int32)


def draw_pair_list(key, part):
    candidates = PLANES * BAND
    candidate = lax.broadcasted_iota(jnp.int32, (candidates,), 0)
    lower_plane = candidate // BAND
    pair_gap = candidate % BAND
    allowed = lower_plane + pair_gap < PLANES
    ceiling = 2147483647 // candidates - 2
    scores = jax.random.randint(key, (candidates,), 0, ceiling) * candidates + candidate
    forced = (candidate == 0) | (candidate == (PLANES - 1) * BAND)
    scores = jnp.where(forced, ceiling * candidates + candidate, scores)
    scores = jnp.where(allowed, scores, -1 - candidate)
    chosen = lax.top_k(scores, PAIRS)[1].astype(jnp.int32)
    return jnp.stack([chosen // BAND, chosen // BAND + chosen % BAND], axis=1).astype(jnp.int32)


def levels(rng, extent, pieces, low, top_value):
    def one(dim, blocks):
        draws = jax.random.uniform(jax.random.fold_in(jax.random.fold_in(rng, 6), dim), (blocks,), jnp.float32, low / len(pieces), top_value / len(pieces))
        return jnp.repeat(jnp.exp(draws), extent[dim] // blocks).reshape((-1,) + (1,) * (len(extent) - dim - 1))

    level = one(*pieces[0])
    for cut in pieces[1:]:
        level = level * one(*cut)
    return level


def scatter_about(own_key, extent, deviation, most, pieces=(), kind=jnp.bfloat16):
    values = deviation * jax.random.normal(own_key, extent, jnp.float32)
    if pieces:
        values = values * levels(own_key, extent, pieces, -0.22, 0.18)
    return jnp.clip(values, -most, most).astype(kind)


def setup_inputs(seed: int = 0) -> dict:
    seeds = jax.random.split(jax.random.key(seed), 4)
    velocity = scatter_about(seeds[0], (PLANES, NX, NZ), 1.0, 6.0, ((0, 4), (1, 8)), jnp.float32)
    plane_slot = draw_plane_slot(jax.random.fold_in(seeds[3], 71), 0)
    pair_list = draw_pair_list(jax.random.fold_in(seeds[3], 71), 0)
    return dict(velocity=velocity, plane_slot=plane_slot, pair_list=pair_list)


def transform_plane(field):
    along_span = jnp.fft.rfft(field, axis=1)[:, :KZ]
    both_ways = jnp.fft.fft(along_span, axis=0)
    both_ways = jnp.concatenate([both_ways[:KX // 2], both_ways[NX - KX // 2:]], axis=0)
    both_ways = jnp.transpose(both_ways) * (1.0 / math.sqrt(NX * NZ))
    return jnp.stack([jnp.real(both_ways), jnp.imag(both_ways)])

def cross_product(first, second):
    real_part = first[..., 0, :, :] * second[..., 0, :, :] + first[..., 1, :, :] * second[..., 1, :, :]
    imag_part = first[..., 1, :, :] * second[..., 0, :, :] - first[..., 0, :, :] * second[..., 1, :, :]
    return jnp.stack([real_part, imag_part], axis=-3)

def reference(velocity, plane_slot, pair_list):
    spectra_slot = lax.map(transform_plane, velocity)
    spectra = jnp.take(spectra_slot, plane_slot, axis=0)
    wanted = jnp.zeros((PLANES, BAND), jnp.int32).at[pair_list[:, 0], pair_list[:, 1] - pair_list[:, 0]].set(1)
    zero_block = jnp.zeros_like(spectra)
    conj_sign = jnp.array([1.0, -1.0], spectra.dtype).reshape(2, 1, 1)
    uppers = []
    lowers = []
    for distance in range(BAND):
        shifted_ahead = jnp.concatenate([spectra[distance:], zero_block[:distance]], axis=0)
        upper_part = jnp.where((wanted[:, distance] == 1)[:, None, None, None], cross_product(spectra, shifted_ahead), 0.0)
        lowers.append(jnp.concatenate([zero_block[:distance], (upper_part * conj_sign)[:PLANES - distance]], axis=0))
        uppers.append(upper_part)
    return (jnp.stack(uppers, axis=1), jnp.stack(lowers, axis=1))
```

```python
import functools
import math

import ml_dtypes
import numpy as np

import jax
import jax.numpy as jnp
from jax import lax
from jax.experimental import pallas as pl
from jax.experimental.pallas import tpu as pltpu
from jax.sharding import PartitionSpec as P

KX = 512
KZ = 1024
F32 = jnp.float32
BF16 = jnp.bfloat16


def split_table(table):
    high = table.astype(np.float32).astype(ml_dtypes.bfloat16)
    low = (table - high.astype(np.float64)).astype(np.float32).astype(ml_dtypes.bfloat16)
    return high, low


def span_tables(nz, shares, chunks):
    per_owner = KZ // shares
    per_chunk = per_owner // chunks
    mode = np.arange(KZ).reshape(shares, chunks, per_chunk // 2, 2)
    mode = mode.transpose(1, 3, 0, 2)
    angle = (mode[..., None] * np.arange(nz // 2) % nz) * (2.0 * math.pi / nz)
    parts = np.stack([np.cos(angle), -np.sin(angle)], axis=2)
    high, low = split_table(parts)
    return np.stack([high, low], axis=2)


def axial_tables(nx, nz, shares):
    pos = np.arange(nx).reshape(shares, nx // shares)
    column = np.arange(KX // 2)
    angle = ((2 * column + 1) * pos[..., None] % (2 * nx)) * (math.pi / nx)
    table = np.concatenate([np.cos(angle), np.sin(angle)], axis=-1) / math.sqrt(nx * nz)
    high, low = split_table(table)
    shift = np.stack([np.cos(pos * math.pi / nx), np.sin(pos * math.pi / nx)], axis=1)
    return np.stack([high, low], axis=1), shift.astype(np.float32)


def halving_orders(shares):
    bits = list(range(1, shares.bit_length() - 1))
    middle = len(bits) // 2
    return bits, bits[middle:] + bits[:middle]


def relative(index, order):
    top = len(order) - 1
    return sum(((index >> (top - step)) & 1) << bit for step, bit in enumerate(order))


def owner_table(shares):
    orders = halving_orders(shares)
    rows = []
    for me in range(shares):
        other = me ^ 1
        sent = [other ^ relative(i, orders[other & 1]) for i in range(shares // 2)]
        kept = [me ^ relative(i, orders[me & 1]) for i in range(shares // 2)]
        rows.append([me] + sent + kept)
    return np.array(rows, np.int32)


def split(value):
    high = value.astype(BF16)
    return high, (value - high.astype(F32)).astype(BF16)


def dot_nt(left, right):
    return lax.dot_general(left, right, (((1,), (1,)), ((), ())), preferred_element_type=F32)


def dot_nn(left, right):
    return lax.dot_general(left, right, (((1,), (0,)), ((), ())), preferred_element_type=F32)


def transform_kernel(planes, rows, shares, meta, field, span, axial, shift, sent, kept, y_high, y_low):
    tile = field.shape[0]
    half = field.shape[1] // 2
    modes = span.shape[5]
    per_part = shares * modes
    step = pl.program_id(0)
    first = field[:, :half]
    second = field[:, half:]
    cos_shift = shift[0, 0:1, :]
    sin_shift = shift[0, 1:2, :]
    for parity in range(2):
        high, low = split(first + second if parity == 0 else first - second)
        table = span[0, parity].reshape(2 * 2 * per_part, half)
        both = dot_nt(table, high)
        value = both[: 2 * per_part] + both[2 * per_part :] + dot_nt(table[: 2 * per_part], low)
        re_part = value[:per_part]
        im_part = value[per_part:]
        turned = (
            re_part * cos_shift - im_part * sin_shift,
            re_part * sin_shift + im_part * cos_shift,
        )
        for part in range(2):
            high, low = split(turned[part])
            y_high[step, parity, part] = high.reshape(shares, modes, tile)
            y_low[step, parity, part] = low.reshape(shares, modes, tile)

    @pl.when(step == pl.num_programs(0) - 1)
    def _():
        half_count = shares // 2
        for plane in range(planes):
            pieces = []
            for index in range(planes * rows // tile):
                start = max(plane * rows, index * tile)
                stop = min((plane + 1) * rows, (index + 1) * tile)
                if start < stop:
                    pieces.append((index, start - index * tile, stop - index * tile))
            for target, base in ((sent, 1), (kept, 1 + half_count)):

                def gather(source):
                    blocks = []
                    for item in range(half_count):
                        owner = meta[base + item]
                        for parity in range(2):
                            for part in range(2):
                                blocks.append(
                                    jnp.concatenate(
                                        [
                                            source[index, parity, part, owner][:, lo:hi]
                                            for index, lo, hi in pieces
                                        ],
                                        axis=1,
                                    )
                                )
                    return jnp.concatenate(blocks, axis=0)

                left = gather(y_high)
                total = dot_nn(left, axial[0, 0]) + dot_nn(left, axial[0, 1])
                total = total + dot_nn(gather(y_low), axial[0, 0])
                target[:, plane] = total.reshape(half_count, 2, 2, modes, KX)


def transform(meta, field, span, axial, shift, chunk, planes):
    shares = axial.shape[0]
    rows = axial.shape[2]
    nz = field.shape[1]
    modes = span.shape[5]
    tile = 256 if rows % 128 == 0 and planes * rows % 256 == 0 else rows
    steps = planes * rows // tile
    out = jax.ShapeDtypeStruct((shares // 2, planes, 2, 2, modes, KX), F32)
    out_spec = pl.BlockSpec(out.shape, lambda i, meta: (0,) * 6)
    table_rows = 4 * shares * modes
    return pl.pallas_call(
        functools.partial(transform_kernel, planes, rows, shares),
        out_shape=(out, out),
        grid_spec=pltpu.PrefetchScalarGridSpec(
            num_scalar_prefetch=1,
            grid=(steps,),
            in_specs=[
                pl.BlockSpec((tile, nz), lambda i, meta: (i, 0)),
                pl.BlockSpec(
                    (1,) + span.shape[1:],
                    lambda i, meta: (chunk, 0, 0, 0, 0, 0, 0),
                    pipeline_mode=pl.Buffered(1),
                ),
                pl.BlockSpec((1,) + axial.shape[1:], lambda i, meta: (meta[0], 0, 0, 0), pipeline_mode=pl.Buffered(1)),
                pl.BlockSpec((1, 2, tile), lambda i, meta: (i, 0, 0)),
            ],
            out_specs=(out_spec, out_spec),
            scratch_shapes=[pltpu.VMEM((steps, 2, 2, shares, modes, tile), BF16)] * 2,
        ),
        compiler_params=pltpu.CompilerParams(vmem_limit_bytes=56 * 1024 * 1024),
        cost_estimate=pl.CostEstimate(
            flops=6 * planes * rows * table_rows * (nz // 2 + KX),
            bytes_accessed=planes * rows * nz * 4 + table_rows * nz * 2 + table_rows * planes * KX * 2,
            transcendentals=0,
        ),
        name="transform",
    )(meta, field, span, axial, shift)


def combine_kernel(count, scalars, *refs):
    terms, out, woven = refs[:count], refs[count], refs[count + 1]
    modes = terms[0].shape[4]
    half = KX // 2
    row = lax.broadcasted_iota(jnp.int32, (half, half), 0)
    column = lax.broadcasted_iota(jnp.int32, (half, half), 1)
    mirror = (row + column == half - 1).astype(BF16)

    def mirrored(value):
        high, rest = split(value)
        middle = value - high.astype(F32)
        middle, low = split(middle)
        return dot_nn(high, mirror) + dot_nn(middle, mirror) + dot_nn(low, mirror)

    for parity in range(2):
        re_rows, im_rows = (
            functools.reduce(lambda a, b: a + b, [term[0, 0, parity, part] for term in terms])
            for part in range(2)
        )
        re_cos, re_sin = re_rows[:, :half], re_rows[:, half:]
        im_cos, im_sin = im_rows[:, :half], im_rows[:, half:]
        values = (
            (re_cos + im_sin, mirrored(re_cos - im_sin)),
            (im_cos - re_sin, mirrored(im_cos + re_sin)),
        )
        for part in range(2):
            for side in range(2):
                for group in range(half // 128):
                    woven[part, side * (half // 128) + group, pl.ds(parity, modes, stride=2), :] = values[part][side][
                        :, group * 128 : (group + 1) * 128
                    ]
    for part in range(2):
        for group in range(KX // 128):
            out[0, part, :, group * 128 : (group + 1) * 128] = woven[part, group]


def combine(scalars, terms, planes):
    modes = terms[0].shape[4]
    spec = pl.BlockSpec(
        (1, 1, 2, 2, modes, KX), lambda i, scalars: (0, scalars[1 + i], 0, 0, 0, 0)
    )
    return pl.pallas_call(
        functools.partial(combine_kernel, len(terms)),
        out_shape=jax.ShapeDtypeStruct((planes, 2, 2 * modes, KX), F32),
        grid_spec=pltpu.PrefetchScalarGridSpec(
            num_scalar_prefetch=1,
            grid=(planes,),
            in_specs=[spec] * len(terms),
            out_specs=pl.BlockSpec((1, 2, 2 * modes, KX), lambda i, scalars: (i, 0, 0, 0)),
            scratch_shapes=[pltpu.VMEM((2, KX // 128, 2 * modes, 128), F32)],
        ),
        cost_estimate=pl.CostEstimate(
            flops=planes * modes * KX * 40, bytes_accessed=planes * modes * KX * 16 * (len(terms) + 1), transcendentals=0
        ),
        name="combine",
    )(scalars, *terms)


def cross_kernel(planes, band, reach, aliased, scalars, pairs, *refs):
    sources = refs[: 1 + 2 * reach]
    band_out, partner_out, wanted = refs[1 + 2 * reach + 2 * aliased :]

    def plane_value(offset):
        if 0 <= offset < planes:
            ref, index = sources[0], offset
        elif offset < 0:
            away = -(offset // planes)
            ref, index = sources[away], offset + away * planes - (1 if away == reach else 0)
        else:
            away = offset // planes
            ref, index = sources[reach + away], offset - away * planes
        return ref[index, 0], ref[index, 1]

    @pl.when(pl.program_id(0) == 0)
    def _():
        first_plane = scalars[0]

        def clear(index, carry):
            wanted[index] = 0
            return carry

        lax.fori_loop(0, 2 * planes * band, clear, 0)

        def mark(index, carry):
            lower = pairs[2 * index]
            upper = pairs[2 * index + 1]
            gap = upper - lower
            for side, plane in enumerate((lower - first_plane, upper - first_plane)):

                @pl.when((plane >= 0) & (plane < planes))
                def _():
                    wanted[(side * planes + plane) * band + gap] = 1

            return carry

        lax.fori_loop(0, pairs.shape[0] // 2, mark, 0)

    values = {offset: plane_value(offset) for offset in range(1 - band, planes + band - 1)}
    for own in range(planes):
        own_re, own_im = values[own]
        for gap in range(band):
            keep = wanted[own * band + gap] != 0
            far_re, far_im = values[own + gap]
            band_out[own, gap, 0] = jnp.where(keep, own_re * far_re + own_im * far_im, 0.0)
            band_out[own, gap, 1] = jnp.where(keep, own_im * far_re - own_re * far_im, 0.0)
            keep = wanted[(planes + own) * band + gap] != 0
            far_re, far_im = values[own - gap]
            partner_out[own, gap, 0] = jnp.where(keep, far_re * own_re + far_im * own_im, 0.0)
            partner_out[own, gap, 1] = jnp.where(keep, far_re * own_im - far_im * own_re, 0.0)


def cross(scalars, pairs, sources, earlier, planes, band, reach, chunk, chunks):
    rows = sources[0].shape[2]
    block = min(rows, 16)
    steps = rows // block
    out = jax.ShapeDtypeStruct((planes, band, 2, chunks * rows, KX), F32)
    out_spec = pl.BlockSpec((planes, band, 2, block, KX), lambda i, *s: (0, 0, 0, chunk * steps + i, 0))
    specs = [pl.BlockSpec((source.shape[0], 2, block, KX), lambda i, *s: (0, 0, i, 0)) for source in sources]
    specs += [pl.BlockSpec(memory_space=pl.ANY)] * len(earlier)
    return pl.pallas_call(
        functools.partial(cross_kernel, planes, band, reach, 1 if earlier else 0),
        out_shape=(out, out),
        grid_spec=pltpu.PrefetchScalarGridSpec(
            num_scalar_prefetch=2,
            grid=(steps,),
            in_specs=specs,
            out_specs=(out_spec, out_spec),
            scratch_shapes=[pltpu.SMEM((2 * planes * band,), jnp.int32)],
        ),
        input_output_aliases={2 + len(sources) + i: i for i in range(len(earlier))},
        cost_estimate=pl.CostEstimate(
            flops=planes * band * rows * KX * 12,
            bytes_accessed=(planes * band * 4 + 2 * (planes + 2 * band)) * rows * KX * 4,
            transcendentals=0,
        ),
        name="cross",
    )(scalars, pairs, *sources, *earlier)


def solution(mesh):
    shares = mesh.shape["pencil"]
    slabs = mesh.shape["plane"]
    reach = slabs // 2
    orders = halving_orders(shares)
    share = KZ // shares
    chunks = 2 if share % 64 == 0 else 1
    core_swap = [(i, i ^ 1) for i in range(shares)]
    swaps = [
        [(i, i ^ (1 << orders[i & 1][step])) for i in range(shares)] for step in range(len(orders[0]))
    ]
    upward = [(i, i + 1) for i in range(slabs - 1)]
    downward = [(i + 1, i) for i in range(slabs - 1)]

    def local(velocity, plane_slot, pair_list):
        planes, rows, nz = velocity.shape
        band = planes * reach
        span = span_tables(nz, shares, chunks)
        axial, shift = axial_tables(rows * shares, nz, shares)
        me = lax.axis_index("pencil")
        meta = lax.dynamic_index_in_dim(jnp.asarray(owner_table(shares)), me, 0, keepdims=False)
        tile = 256 if rows % 128 == 0 and planes * rows % 256 == 0 else rows
        mine = lax.dynamic_index_in_dim(jnp.asarray(shift), me, 0, keepdims=False)
        mine = jnp.tile(mine, (1, planes)).reshape(2, planes * rows // tile, tile).transpose(1, 0, 2)
        first_plane = lax.axis_index("plane") * planes
        held = lax.dynamic_slice_in_dim(plane_slot, first_plane, planes, 0) - first_plane
        scalars = jnp.concatenate([first_plane[None], held]).astype(jnp.int32)
        pairs = pair_list.reshape(-1)
        field = velocity.reshape(planes * rows, nz)

        def reduced(chunk):
            sent, kept = transform(meta, field, span, axial, mine, chunk, planes)
            terms = [kept, lax.ppermute(sent, "pencil", core_swap)]
            count = shares // 2
            for swap in swaps:
                count //= 2
                leaving = functools.reduce(lambda a, b: a + b, [term[count : 2 * count] for term in terms])
                terms.append(lax.ppermute(leaving, "pencil", swap))
            return combine(scalars, terms, planes)

        outputs = ()
        for chunk in range(chunks):
            own = reduced(chunk)
            below, above = [own], [own]
            for away in range(1, reach + 1):
                last = away == reach
                low, high = below[-1], above[-1]
                below.append(lax.ppermute(low[1:] if last else low, "plane", upward))
                above.append(lax.ppermute(high[:-1] if last else high, "plane", downward))
            outputs = cross(
                scalars, pairs, below + above[1:], outputs, planes, band, reach, chunk, chunks
            )
        return tuple(outputs)

    return jax.shard_map(
        local,
        mesh=mesh,
        in_specs=(P("plane", "pencil", None), P(), P()),
        out_specs=(P("plane", None, None, "pencil", None), P("plane", None, None, "pencil", None)),
        check_vma=False,
    )
```

```python
import functools
import math

import ml_dtypes
import numpy as np

import jax
import jax.numpy as jnp
from jax import lax
from jax.experimental import pallas as pl
from jax.experimental.pallas import tpu as pltpu
from jax.sharding import PartitionSpec as P

KX = 512
KZ = 1024
LANES = 128
GROUP = 8
F32 = jnp.float32
BF16 = jnp.bfloat16


def split_table(table):
    high = table.astype(np.float32).astype(ml_dtypes.bfloat16)
    low = (table - high.astype(np.float64)).astype(np.float32).astype(ml_dtypes.bfloat16)
    return high, low


def class_pairs(radix):
    return [(0, radix // 2)] + [(k, radix - k) for k in range(1, radix // 2)]


def span_table(nz, shares, radix):
    length = nz // radix
    padded = -(-length // LANES) * LANES
    per_owner = KZ // shares
    place = np.arange(length)
    pairs = []
    for number, pair in enumerate(class_pairs(radix)):
        table = np.zeros((2, shares, 2, GROUP, 2, padded))
        for member, residue in enumerate(pair):
            mode = np.arange(shares)[:, None] * per_owner + residue + radix * np.arange(GROUP)
            angle = (mode[..., None] * place % nz) * (2.0 * math.pi / nz)
            cosine, sine = np.cos(angle), np.sin(angle)
            if number == 0:
                table[0, :, member, :, member, :length] = cosine
                table[1, :, member, :, member, :length] = -sine
            else:
                sign = 1.0 if member == 0 else -1.0
                table[0, :, member, :, 0, :length] = cosine
                table[0, :, member, :, 1, :length] = sign * sine
                table[1, :, member, :, 0, :length] = -sine
                table[1, :, member, :, 1, :length] = sign * cosine
        pairs.append(table.reshape(2 * shares * 2 * GROUP, 2 * padded))
    high, low = split_table(np.stack(pairs))
    return np.concatenate([high, low], axis=1)


def axial_table(nx, nz, shares):
    pos = np.arange(nx).reshape(shares, nx // shares)
    column = np.arange(KX // 2)
    angle = ((2 * column + 1) * pos[..., None] % (2 * nx)) * (math.pi / nx)
    both = np.stack([np.cos(angle), np.sin(angle)], axis=2) / math.sqrt(nx * nz)
    both = both.reshape(shares, nx // shares, 2, -1, LANES).transpose(0, 1, 3, 2, 4)
    high, low = split_table(both.reshape(shares, nx // shares, KX))
    return np.concatenate([high, high, low], axis=1)


def shift_table(nx, shares):
    angle = np.arange(nx).reshape(shares, 1, nx // shares) * (math.pi / nx)
    rest = np.zeros((shares, 6, nx // shares))
    return np.concatenate([np.cos(angle), np.sin(angle), rest], axis=1).astype(np.float32)


def halving_orders(shares):
    bits = list(range(1, shares.bit_length() - 1))
    middle = len(bits) // 2
    return bits, bits[middle:] + bits[:middle]


def relative(index, order):
    top = len(order) - 1
    return sum(((index >> (top - step)) & 1) << bit for step, bit in enumerate(order))


def place_table(shares):
    orders = halving_orders(shares)
    rows = []
    for me in range(shares):
        other = me ^ 1
        sent = [other ^ relative(i, orders[other & 1]) for i in range(shares // 2)]
        kept = [me ^ relative(i, orders[me & 1]) for i in range(shares // 2)]
        rows.append(np.argsort(sent + kept))
    return np.array(rows, np.int32)


def split(value):
    high = value.astype(BF16)
    return high, (value - high.astype(F32)).astype(BF16)


def dot_nt(left, right):
    return lax.dot_general(left, right, (((1,), (1,)), ((), ())), preferred_element_type=F32)


def dot_nn(left, right):
    return lax.dot_general(left, right, (((1,), (0,)), ((), ())), preferred_element_type=F32)


def real_dft(values):
    count = len(values)
    if count == 1:
        return [(values[0], None)]
    if count == 2:
        return [(values[0] + values[1], None), (values[0] - values[1], None)]
    even = real_dft(values[0::2])
    odd = real_dft(values[1::2])
    out = [None] * (count // 2 + 1)
    for k in range(count // 4 + 1):
        even_re, even_im = even[k]
        odd_re, odd_im = odd[k]
        if k == 0:
            out[0] = (even_re + odd_re, None)
            out[count // 2] = (even_re - odd_re, None)
        elif 4 * k == count:
            out[k] = (even_re, -odd_re)
        else:
            cosine = math.cos(2.0 * math.pi * k / count)
            sine = math.sin(2.0 * math.pi * k / count)
            if 8 * k == count:
                turned_re = (odd_re + odd_im) * cosine
                turned_im = (odd_im - odd_re) * cosine
            else:
                turned_re = odd_re * cosine + odd_im * sine
                turned_im = odd_im * cosine - odd_re * sine
            out[k] = (even_re + turned_re, even_im + turned_im)
            out[count // 2 - k] = (even_re - turned_re, turned_im - even_im)
    return out


def fold_strip(radix, field, rows, fold_high, fold_low):
    nz = field.shape[1]
    length = nz // radix
    padded = -(-length // LANES) * LANES
    for piece in range(padded // LANES):
        blocks = []
        for block in range(radix):
            start = block * length + piece * LANES
            offset = start % LANES
            base = start - offset
            if offset == 0:
                blocks.append(field[rows, base : base + LANES])
            else:
                stop = min(base + 2 * LANES, nz)
                blocks.append(pltpu.roll(field[rows, base:stop], stop - base - offset, 1)[:, :LANES])
        waves = real_dft(blocks)
        for number, pair in enumerate(class_pairs(radix)):
            parts = (waves[0][0], waves[radix // 2][0]) if number == 0 else waves[pair[0]]
            for part in range(2):
                high, low = split(parts[part])
                columns = slice(part * padded + piece * LANES, part * padded + (piece + 1) * LANES)
                fold_high[number, rows, columns] = high
                fold_low[number, rows, columns] = low


def plane_kernel(radix, plane, places, plane_slot, field, table, axial, shift, sent, kept, *scratch):
    velocity, span, wave, turn, fold_high, fold_low, y, total, load_done, rest_done, out_done = scratch
    planes, rows, _ = field.shape
    half_count, count, _ = sent.shape
    shares = 2 * half_count
    me = lax.axis_index("pencil")
    first_plane = lax.axis_index("plane") * planes
    slot = plane_slot[first_plane + plane] - first_plane
    strip = 16
    cut = rows // load_done.shape[0]
    loads = []
    for piece in range(rows // cut):
        part = pl.ds(piece * cut, cut)
        loads.append(pltpu.make_async_copy(field.at[slot, part], velocity.at[part], load_done.at[piece]))
    rest = [
        pltpu.make_async_copy(source, target, rest_done.at[index])
        for index, (source, target) in enumerate(((table, span), (shift.at[me], turn), (axial.at[me], wave)))
    ]
    loads[0].start()
    for copy in rest:
        copy.start()
    for copy in loads[1:]:
        copy.start()
    for piece in range(rows // cut):
        loads[piece].wait()

        def fold(index, carry):
            first = pl.multiple_of(piece * cut + index * strip, strip)
            fold_strip(radix, velocity, pl.ds(first, strip), fold_high, fold_low)
            return carry

        lax.fori_loop(0, cut // strip, fold, 0, unroll=2)
    rest[0].wait()
    rest[1].wait()
    cos_shift = turn[0:1, :]
    sin_shift = turn[1:2, :]
    half = shares * 2 * GROUP
    for number in range(radix // 2):
        both = dot_nt(span[number], fold_high[number])
        value = both[: 2 * half] + both[2 * half :] + dot_nt(span[number, : 2 * half], fold_low[number])
        re_part = value[:half]
        im_part = value[half:]
        turned = (
            re_part * cos_shift - im_part * sin_shift,
            re_part * sin_shift + im_part * cos_shift,
        )
        for part in range(2):
            high, low = split(turned[part])
            first = (number * 2 + part) * 2 * GROUP
            for owner in range(shares):
                place = places[me * shares + owner]
                owned = slice(owner * 2 * GROUP, (owner + 1) * 2 * GROUP)
                y[place, first : first + 2 * GROUP, :rows] = high[owned]
                y[place, first : first + 2 * GROUP, rows:] = low[owned]
    rest[2].wait()
    owners = 2 if half_count % 2 == 0 else 1
    leaving = []
    for first in range(0, shares, owners):
        left = y[first : first + owners].reshape(owners * count, 2 * rows)
        value = dot_nn(left, wave[: 2 * rows]) + dot_nn(left[:, :rows], wave[2 * rows :])
        window = pl.ds(first, owners)
        total[window] = value.reshape(owners, count, KX)
        target = sent.at[window] if first < half_count else kept.at[pl.ds(first - half_count, owners)]
        leaving.append(pltpu.make_async_copy(total.at[window], target, out_done.at[first // owners]))
        leaving[-1].start()
    for copy in leaving:
        copy.wait()


def transform_plane(plane, places, plane_slot, field, table, axial, shift, radix):
    planes, rows, nz = field.shape
    shares = axial.shape[0]
    half_count = shares // 2
    pairs, table_rows, depth = table.shape
    count = pairs * 4 * GROUP
    out = jax.ShapeDtypeStruct((half_count, count, KX), F32)
    pieces = rows // LANES if rows % LANES == 0 else 1
    smem = pl.BlockSpec(memory_space=pltpu.SMEM)
    hbm = pl.BlockSpec(memory_space=pl.ANY)
    return pl.pallas_call(
        functools.partial(plane_kernel, radix, plane),
        out_shape=(out, out),
        in_specs=[smem, smem, hbm, hbm, hbm, hbm],
        out_specs=(hbm, hbm),
        scratch_shapes=[
            pltpu.VMEM((rows, nz), F32),
            pltpu.VMEM(table.shape, BF16),
            pltpu.VMEM(axial.shape[1:], BF16),
            pltpu.VMEM(shift.shape[1:], F32),
            pltpu.VMEM((pairs, rows, depth), BF16),
            pltpu.VMEM((pairs, rows, depth), BF16),
            pltpu.VMEM((shares, count, 2 * rows), BF16),
            pltpu.VMEM((shares, count, KX), F32),
            pltpu.SemaphoreType.DMA((pieces,)),
            pltpu.SemaphoreType.DMA((3,)),
            pltpu.SemaphoreType.DMA((shares,)),
        ],
        compiler_params=pltpu.CompilerParams(vmem_limit_bytes=56 * 1024 * 1024),
        cost_estimate=pl.CostEstimate(
            flops=3 * rows * pairs * table_rows * depth + 6 * shares * count * rows * KX,
            bytes_accessed=rows * nz * 4 + pairs * table_rows * depth * 2 + shares * count * KX * 4,
            transcendentals=0,
        ),
        name="plane",
    )(places, plane_slot, field, table, axial, shift)


def cross_kernel(radix, planes, offsets, band_slots, partner_slots, pairs, *refs):
    sources = dict(zip(offsets, refs[: len(offsets)]))
    band_out, partner_out, wanted, woven = refs[-4:]
    band = wanted.shape[0] // (2 * planes)
    share = woven.shape[2]
    side = pl.program_id(1)

    @pl.when((pl.program_id(0) == 0) & (side == 0))
    def _():
        first_plane = lax.axis_index("plane") * planes

        def clear(index, carry):
            wanted[index] = 0
            return carry

        lax.fori_loop(0, 2 * planes * band, clear, 0)

        def mark(index, carry):
            lower = pairs[index, 0]
            upper = pairs[index, 1]
            for end, plane in enumerate((lower - first_plane, upper - first_plane)):

                @pl.when((plane >= 0) & (plane < planes))
                def _():
                    wanted[(end * planes + plane) * band + upper - lower] = 1

            return carry

        lax.fori_loop(0, pairs.shape[0], mark, 0)

    residues = [residue for pair in class_pairs(radix) for residue in pair]

    def parts(source):
        value = source[0].reshape(radix // 2, 2, 2 * GROUP, 2 * LANES)
        re_rows = value[:, 0].reshape(share, 2 * LANES)
        im_rows = value[:, 1].reshape(share, 2 * LANES)
        return re_rows[:, :LANES], re_rows[:, LANES:], im_rows[:, :LANES], im_rows[:, LANES:]

    def weave(index, values):
        for part in range(2):
            for number, residue in enumerate(residues):
                woven[index, part, pl.ds(residue, GROUP, stride=radix), :] = values[part][
                    number * GROUP : (number + 1) * GROUP
                ]

    @pl.when(side == 0)
    def _():
        for index, offset in enumerate(offsets):
            re_cos, re_sin, im_cos, im_sin = parts(sources[offset])
            weave(index, (re_cos + im_sin, im_cos - re_sin))

    @pl.when(side == 1)
    def _():
        row = lax.broadcasted_iota(jnp.int32, (LANES, LANES), 0)
        column = lax.broadcasted_iota(jnp.int32, (LANES, LANES), 1)
        mirror = (row + column == LANES - 1).astype(BF16)

        def mirrored(value):
            high = value.astype(BF16)
            middle, low = split(value - high.astype(F32))
            return dot_nn(high, mirror) + dot_nn(middle, mirror) + dot_nn(low, mirror)

        for index, offset in enumerate(offsets):
            re_cos, re_sin, im_cos, im_sin = parts(sources[offset])
            weave(index, (mirrored(re_cos - im_sin), mirrored(im_cos + re_sin)))

    def spectrum(offset):
        index = offsets.index(offset)
        return woven[index, 0], woven[index, 1]

    for out, slots, end in ((band_out, band_slots, 0), (partner_out, partner_slots, 1)):
        for place, own, gap in slots:
            keep = wanted[(end * planes + own) * band + gap] != 0
            own_re, own_im = spectrum(own)
            if end == 0:
                far_re, far_im = spectrum(own + gap)
                imag = own_im * far_re - own_re * far_im
            else:
                far_re, far_im = spectrum(own - gap)
                imag = far_re * own_im - far_im * own_re
            out[place + (0,)] = jnp.where(keep, own_re * far_re + own_im * far_im, 0.0)
            out[place + (1,)] = jnp.where(keep, imag, 0.0)


def cross(pairs, sources, earlier, planes, band, radix, last):
    share = radix * GROUP
    blocks = KX // 2 // LANES
    out = jax.ShapeDtypeStruct((planes, band, 2, share, KX), F32)

    def lane_block(block, side):
        return block + side * (2 * blocks - 1 - 2 * block)

    slots = {0: [], 1: []}
    if last:
        places = {0: (planes - 1, band - 1), 1: (0, band - 1)}
        slots = {0: [((0, 0), planes - 1, band - 1)], 1: [((0, 0), 0, band - 1)]}
        out_specs = tuple(
            pl.BlockSpec(
                (1, 1, 2, share, LANES),
                functools.partial(lambda end, b, side: places[end] + (0, 0, lane_block(b, side)), end),
            )
            for end in range(2)
        )
    else:
        for own in range(planes):
            for gap in range(band):
                for end in range(2):
                    far = own + gap if end == 0 else own - gap
                    if far in sources:
                        slots[end].append(((own, gap), own, gap))
        spec = pl.BlockSpec(
            (planes, band, 2, share, LANES), lambda b, side: (0, 0, 0, 0, lane_block(b, side))
        )
        out_specs = (spec, spec)
    used = sorted(
        {own for end in range(2) for _, own, _ in slots[end]}
        | {own + gap for _, own, gap in slots[0]}
        | {own - gap for _, own, gap in slots[1]}
    )
    specs = [pl.BlockSpec(memory_space=pltpu.SMEM)]
    specs += [pl.BlockSpec((1, 2 * share, 2 * LANES), lambda b, side: (0, 0, b))] * len(used)
    specs += [pl.BlockSpec(memory_space=pl.ANY)] * len(earlier)
    return pl.pallas_call(
        functools.partial(cross_kernel, radix, planes, used, slots[0], slots[1]),
        out_shape=(out, out),
        grid=(blocks, 2),
        in_specs=specs,
        out_specs=out_specs,
        scratch_shapes=[
            pltpu.SMEM((2 * planes * band,), jnp.int32),
            pltpu.VMEM((len(used), 2, share, LANES), F32),
        ],
        input_output_aliases={1 + len(used) + i: i for i in range(len(earlier))},
        compiler_params=pltpu.CompilerParams(vmem_limit_bytes=48 * 1024 * 1024),
        cost_estimate=pl.CostEstimate(
            flops=(len(slots[0]) + len(slots[1])) * share * KX * 6 + len(used) * share * KX * 200,
            bytes_accessed=(len(slots[0]) + len(slots[1]) + len(used)) * share * KX * 8,
            transcendentals=0,
        ),
        name="cross",
    )(pairs, *[sources[offset] for offset in used], *earlier)


def solution(mesh):
    shares = mesh.shape["pencil"]
    slabs = mesh.shape["plane"]
    reach = slabs // 2
    orders = halving_orders(shares)
    radix = KZ // shares // GROUP
    core_swap = [(i, i ^ 1) for i in range(shares)]
    swaps = [
        [(i, i ^ (1 << orders[i & 1][step])) for i in range(shares)] for step in range(len(orders[0]))
    ]
    upward = [(i, i + 1) for i in range(slabs - 1)]
    downward = [(i + 1, i) for i in range(slabs - 1)]

    def local(velocity, plane_slot, pair_list):
        planes, rows, nz = velocity.shape
        band = planes * reach
        table = span_table(nz, shares, radix)
        axial = axial_table(rows * shares, nz, shares)
        shift = shift_table(rows * shares, shares)
        places = place_table(shares).reshape(-1)

        def after(value, *earlier):
            return lax.optimization_barrier((value,) + earlier)[0]

        near, far = {}, {}
        gates = {}
        for plane in range(planes):
            sent, kept = transform_plane(
                plane, places, plane_slot, velocity, table, axial, shift, radix
            )
            terms = [kept, lax.ppermute(sent, "pencil", core_swap)]
            count = shares // 2
            first_hops = []
            for step, swap in enumerate(swaps):
                count //= 2
                leaving = functools.reduce(lambda a, b: a + b, [term[count : 2 * count] for term in terms])
                if plane:
                    leaving = after(leaving, *gates["sum" if step == 0 else "hop"])
                if step == 0:
                    gates["core"] = leaving
                terms.append(lax.ppermute(leaving, "pencil", swap))
                if step == 0:
                    gates["sum"] = [terms[-1]]
            near[plane] = functools.reduce(lambda a, b: a + b, [term[:1] for term in terms])
            below, above = near[plane], near[plane]
            for away in range(1, reach + 1):
                home = near if away < reach else far
                if away < reach or plane > 0:
                    if away == reach and far:
                        below = after(below, *far.values())
                    below = lax.ppermute(below, "plane", upward)
                    home[plane - away * planes] = below
                    first_hops.append(below)
                if away < reach or plane < planes - 1:
                    above = lax.ppermute(above, "plane", downward)
                    home[plane + away * planes] = above
                    first_hops.append(above)
            gates["hop"] = first_hops[:2]
        outputs = cross(pair_list, near, (), planes, band, radix, False)
        return tuple(cross(pair_list, {**near, **far}, outputs, planes, band, radix, True))

    return jax.shard_map(
        local,
        mesh=mesh,
        in_specs=(P("plane", "pencil", None), P(), P()),
        out_specs=(P("plane", None, None, "pencil", None), P("plane", None, None, "pencil", None)),
        check_vma=False,
    )
```

```python
import functools
import math

import ml_dtypes
import numpy as np

import jax
import jax.numpy as jnp
from jax import lax
from jax.experimental import pallas as pl
from jax.experimental.pallas import tpu as pltpu
from jax.sharding import PartitionSpec as P

KX = 512
KZ = 1024
LANES = 128
GROUP = 8
VMEM_LIMIT = 56 * 1024 * 1024
F32 = jnp.float32
BF16 = jnp.bfloat16


def split_table(table):
    high = table.astype(np.float32).astype(ml_dtypes.bfloat16)
    low = (table - high.astype(np.float64)).astype(np.float32).astype(ml_dtypes.bfloat16)
    return high, low


def class_pairs(radix):
    return [(0, radix // 2)] + [(k, radix - k) for k in range(1, radix // 2)]


def span_table(nz, shares, radix):
    length = nz // radix
    padded = -(-length // LANES) * LANES
    per_owner = KZ // shares
    place = np.arange(length)
    pairs = []
    for number, pair in enumerate(class_pairs(radix)):
        table = np.zeros((2, shares, 2, GROUP, 2, padded))
        for member, residue in enumerate(pair):
            mode = np.arange(shares)[:, None] * per_owner + residue + radix * np.arange(GROUP)
            angle = (mode[..., None] * place % nz) * (2.0 * math.pi / nz)
            cosine, sine = np.cos(angle), np.sin(angle)
            if number == 0:
                table[0, :, member, :, member, :length] = cosine
                table[1, :, member, :, member, :length] = -sine
            else:
                sign = 1.0 if member == 0 else -1.0
                table[0, :, member, :, 0, :length] = cosine
                table[0, :, member, :, 1, :length] = sign * sine
                table[1, :, member, :, 0, :length] = -sine
                table[1, :, member, :, 1, :length] = sign * cosine
        pairs.append(table.reshape(2 * shares * 2 * GROUP, 2 * padded))
    high, low = split_table(np.stack(pairs))
    return np.concatenate([high, low], axis=1)


def axial_table(nx, nz, shares):
    pos = np.arange(nx).reshape(shares, nx // shares)
    column = np.arange(KX // 2)
    angle = ((2 * column + 1) * pos[..., None] % (2 * nx)) * (math.pi / nx)
    both = np.stack([np.cos(angle), np.sin(angle)], axis=2) / math.sqrt(nx * nz)
    both = both.reshape(shares, nx // shares, 2, -1, LANES).transpose(0, 1, 3, 2, 4)
    high, low = split_table(both.reshape(shares, nx // shares, KX))
    return np.concatenate([high, high, low], axis=1)


def shift_table(nx, shares):
    angle = np.arange(nx).reshape(shares, 1, nx // shares) * (math.pi / nx)
    rest = np.zeros((shares, 6, nx // shares))
    return np.concatenate([np.cos(angle), np.sin(angle), rest], axis=1).astype(np.float32)


def halving_orders(shares):
    bits = list(range(1, shares.bit_length() - 1))
    middle = len(bits) // 2
    return bits, bits[middle:] + bits[:middle]


def relative(index, order):
    top = len(order) - 1
    return sum(((index >> (top - step)) & 1) << bit for step, bit in enumerate(order))


def place_table(shares):
    orders = halving_orders(shares)
    rows = []
    for me in range(shares):
        other = me ^ 1
        sent = [other ^ relative(i, orders[other & 1]) for i in range(shares // 2)]
        kept = [me ^ relative(i, orders[me & 1]) for i in range(shares // 2)]
        rows.append(np.argsort(sent + kept))
    return np.array(rows, np.int32)


def split(value):
    high = value.astype(BF16)
    return high, (value - high.astype(F32)).astype(BF16)


def dot_nt(left, right):
    return lax.dot_general(left, right, (((1,), (1,)), ((), ())), preferred_element_type=F32)


def dot_nn(left, right):
    return lax.dot_general(left, right, (((1,), (0,)), ((), ())), preferred_element_type=F32)


def real_dft(values):
    count = len(values)
    if count == 1:
        return [(values[0], None)]
    if count == 2:
        return [(values[0] + values[1], None), (values[0] - values[1], None)]
    even = real_dft(values[0::2])
    odd = real_dft(values[1::2])
    out = [None] * (count // 2 + 1)
    for k in range(count // 4 + 1):
        even_re, even_im = even[k]
        odd_re, odd_im = odd[k]
        if k == 0:
            out[0] = (even_re + odd_re, None)
            out[count // 2] = (even_re - odd_re, None)
        elif 4 * k == count:
            out[k] = (even_re, -odd_re)
        else:
            cosine = math.cos(2.0 * math.pi * k / count)
            sine = math.sin(2.0 * math.pi * k / count)
            if 8 * k == count:
                turned_re = (odd_re + odd_im) * cosine
                turned_im = (odd_im - odd_re) * cosine
            else:
                turned_re = odd_re * cosine + odd_im * sine
                turned_im = odd_im * cosine - odd_re * sine
            out[k] = (even_re + turned_re, even_im + turned_im)
            out[count // 2 - k] = (even_re - turned_re, turned_im - even_im)
    return out


def fold_strip(radix, field, rows, fold_high, fold_low):
    nz = field.shape[1]
    length = nz // radix
    padded = -(-length // LANES) * LANES
    for piece in range(padded // LANES):
        blocks = []
        for block in range(radix):
            start = block * length + piece * LANES
            offset = start % LANES
            base = start - offset
            if offset == 0:
                blocks.append(field[rows, base : base + LANES])
            else:
                stop = min(base + 2 * LANES, nz)
                blocks.append(pltpu.roll(field[rows, base:stop], stop - base - offset, 1)[:, :LANES])
        waves = real_dft(blocks)
        for number, pair in enumerate(class_pairs(radix)):
            parts = (waves[0][0], waves[radix // 2][0]) if number == 0 else waves[pair[0]]
            for part in range(2):
                high, low = split(parts[part])
                columns = slice(part * padded + piece * LANES, part * padded + (piece + 1) * LANES)
                fold_high[number, rows, columns] = high
                fold_low[number, rows, columns] = low


def start_all(copies):
    for copy in copies:
        copy.start()


def span_phase(radix, plane, places, plane_slot, field, table, shift, y, scratch, after_pair):
    velocity, span, turn, fold_high, fold_low, load_done, rest_done = scratch
    planes, rows, _ = field.shape
    shares = y.shape[0]
    me = lax.axis_index("pencil")
    first_plane = lax.axis_index("plane") * planes
    slot = plane_slot[first_plane + plane] - first_plane
    strip = 16
    cut = rows // load_done.shape[0]
    loads = []
    for piece in range(rows // cut):
        part = pl.ds(piece * cut, cut)
        loads.append(pltpu.make_async_copy(field.at[slot, part], velocity.at[part], load_done.at[piece]))
    rest = [
        pltpu.make_async_copy(table, span, rest_done.at[0]),
        pltpu.make_async_copy(shift.at[me], turn, rest_done.at[1]),
    ]
    start_all(loads)
    start_all(rest)
    yield
    for piece in range(rows // cut):
        loads[piece].wait()

        def fold(index, carry):
            first = pl.multiple_of(piece * cut + index * strip, strip)
            fold_strip(radix, velocity, pl.ds(first, strip), fold_high, fold_low)
            return carry

        lax.fori_loop(0, cut // strip, fold, 0, unroll=8 if cut % (8 * strip) == 0 else 2)
    for copy in rest:
        copy.wait()
    cos_shift = turn[0:1, :]
    sin_shift = turn[1:2, :]
    half = shares * 2 * GROUP
    for number in range(radix // 2):
        both = dot_nt(span[number], fold_high[number])
        value = both[: 2 * half] + both[2 * half :] + dot_nt(span[number, : 2 * half], fold_low[number])
        re_part = value[:half]
        im_part = value[half:]
        turned = (
            re_part * cos_shift - im_part * sin_shift,
            re_part * sin_shift + im_part * cos_shift,
        )
        for part in range(2):
            high, low = split(turned[part])
            first = (number * 2 + part) * 2 * GROUP
            for owner in range(shares):
                place = places[me * shares + owner]
                owned = slice(owner * 2 * GROUP, (owner + 1) * 2 * GROUP)
                y[place, first : first + 2 * GROUP, :rows] = high[owned]
                y[place, first : first + 2 * GROUP, rows:] = low[owned]
        after_pair(number)
    yield


def axial_phase(y, wave, total, sent, kept, out_done, before_group):
    shares, count, width = y.shape
    half_count = shares // 2
    rows = width // 2
    owners = shares // out_done.shape[0]
    leaving = []
    for first in range(0, shares, owners):
        before_group(first // owners)
        left = y[first : first + owners].reshape(owners * count, width)
        value = dot_nn(left, wave[:width]) + dot_nn(left[:, :rows], wave[width:])
        window = pl.ds(first, owners)
        total[window] = value.reshape(owners, count, KX)
        target = sent.at[window] if first < half_count else kept.at[pl.ds(first - half_count, owners)]
        leaving.append(pltpu.make_async_copy(total.at[window], target, out_done.at[first // owners]))
        leaving[-1].start()
    for copy in leaving:
        copy.wait()


def whole_kernel(radix, plane, places, plane_slot, field, table, shift, axial, sent, kept, y, wave, total, wave_done, out_done, *scratch):
    phase = span_phase(radix, plane, places, plane_slot, field, table, shift, y, scratch, lambda number: None)
    next(phase)
    load = pltpu.make_async_copy(axial.at[lax.axis_index("pencil")], wave, wave_done)
    load.start()
    next(phase)
    load.wait()
    axial_phase(y, wave, total, sent, kept, out_done, lambda group: None)


def span_kernel(radix, plane, places, plane_slot, field, table, shift, y_out, y, pair_done, *scratch):
    height = y.shape[1] // (radix // 2)
    copies = [
        pltpu.make_async_copy(
            y.at[:, pl.ds(number * height, height)], y_out.at[:, pl.ds(number * height, height)], pair_done.at[number]
        )
        for number in range(radix // 2)
    ]
    for _ in span_phase(
        radix, plane, places, plane_slot, field, table, shift, y, scratch, lambda number: copies[number].start()
    ):
        pass
    for copy in copies:
        copy.wait()


def axial_kernel(y_in, axial, sent, kept, y, wave, total, wave_done, out_done, in_done):
    owners = y.shape[0] // out_done.shape[0]
    load = pltpu.make_async_copy(axial.at[lax.axis_index("pencil")], wave, wave_done)
    load.start()
    copies = []
    for group in range(out_done.shape[0]):
        window = pl.ds(group * owners, owners)
        copies.append(pltpu.make_async_copy(y_in.at[window], y.at[window], in_done.at[group]))
    start_all(copies)
    load.wait()
    axial_phase(y, wave, total, sent, kept, out_done, lambda group: copies[group].wait())


def transform_calls(planes, rows, nz, shares, radix):
    table = span_table(nz, shares, radix)
    axial = axial_table(rows * shares, nz, shares)
    shift = shift_table(rows * shares, shares)
    places = place_table(shares).reshape(-1)
    half_count = shares // 2
    pairs, table_rows, depth = table.shape
    count = pairs * 4 * GROUP
    owners = 2 if half_count % 2 == 0 else 1
    pieces = rows // LANES if rows % LANES == 0 else 1
    out = jax.ShapeDtypeStruct((half_count, count, KX), F32)
    modes = jax.ShapeDtypeStruct((shares, count, 2 * rows), BF16)
    smem = pl.BlockSpec(memory_space=pltpu.SMEM)
    hbm = pl.BlockSpec(memory_space=pl.ANY)
    one, many = pltpu.SemaphoreType.DMA(()), lambda number: pltpu.SemaphoreType.DMA((number,))
    y = pltpu.VMEM(modes.shape, BF16)
    span_scratch = [
        pltpu.VMEM((rows, nz), F32),
        pltpu.VMEM(table.shape, BF16),
        pltpu.VMEM(shift.shape[1:], F32),
        pltpu.VMEM((pairs, rows, depth), BF16),
        pltpu.VMEM((pairs, rows, depth), BF16),
        many(pieces),
        many(2),
    ]
    axial_scratch = [
        pltpu.VMEM(axial.shape[1:], BF16),
        pltpu.VMEM((shares, count, KX), F32),
        one,
        many(shares // owners),
    ]
    span_cost = (3 * rows * pairs * table_rows * depth, rows * nz * 4 + pairs * table_rows * depth * 2)
    axial_cost = (6 * shares * count * rows * KX, shares * count * (KX + rows) * 4)

    def call(kernel, name, costs, ins, outs, scratch):
        return pl.pallas_call(
            kernel,
            out_shape=outs,
            in_specs=ins,
            out_specs=jax.tree.map(lambda _: hbm, outs),
            scratch_shapes=scratch,
            compiler_params=pltpu.CompilerParams(vmem_limit_bytes=VMEM_LIMIT),
            cost_estimate=pl.CostEstimate(
                flops=sum(cost[0] for cost in costs), bytes_accessed=sum(cost[1] for cost in costs), transcendentals=0
            ),
            name=name,
        )

    def whole(plane, plane_slot, field):
        return call(
            functools.partial(whole_kernel, radix, plane),
            "whole",
            [span_cost, axial_cost],
            [smem, smem, hbm, hbm, hbm, hbm],
            (out, out),
            [y] + axial_scratch + span_scratch,
        )(places, plane_slot, field, table, shift, axial)

    def span(plane, plane_slot, field):
        return call(
            functools.partial(span_kernel, radix, plane),
            "span",
            [span_cost],
            [smem, smem, hbm, hbm, hbm],
            modes,
            [y, many(pairs)] + span_scratch,
        )(places, plane_slot, field, table, shift)

    def along_x(spanned):
        return call(
            axial_kernel,
            "axial",
            [axial_cost],
            [hbm, hbm],
            (out, out),
            [y] + axial_scratch + [many(shares // owners)],
        )(spanned, axial)

    return whole, span, along_x


def cross_kernel(radix, planes, offsets, band_slots, partner_slots, pairs, *refs):
    sources = dict(zip(offsets, refs[: len(offsets)]))
    band_out, partner_out, wanted, woven = refs[-4:]
    band = wanted.shape[0] // (2 * planes)
    share = woven.shape[2]
    side = pl.program_id(1)

    @pl.when((pl.program_id(0) == 0) & (side == 0))
    def _():
        first_plane = lax.axis_index("plane") * planes

        def clear(index, carry):
            wanted[index] = 0
            return carry

        lax.fori_loop(0, 2 * planes * band, clear, 0)

        def mark(index, carry):
            lower = pairs[index, 0]
            upper = pairs[index, 1]
            for end, plane in enumerate((lower - first_plane, upper - first_plane)):

                @pl.when((plane >= 0) & (plane < planes))
                def _():
                    wanted[(end * planes + plane) * band + upper - lower] = 1

            return carry

        lax.fori_loop(0, pairs.shape[0], mark, 0)

    residues = [residue for pair in class_pairs(radix) for residue in pair]

    def parts(source):
        value = source[0].reshape(radix // 2, 2, 2 * GROUP, 2 * LANES)
        re_rows = value[:, 0].reshape(share, 2 * LANES)
        im_rows = value[:, 1].reshape(share, 2 * LANES)
        return re_rows[:, :LANES], re_rows[:, LANES:], im_rows[:, :LANES], im_rows[:, LANES:]

    def weave(index, values):
        for part in range(2):
            for number, residue in enumerate(residues):
                woven[index, part, pl.ds(residue, GROUP, stride=radix), :] = values[part][
                    number * GROUP : (number + 1) * GROUP
                ]

    @pl.when(side == 0)
    def _():
        for index, offset in enumerate(offsets):
            re_cos, re_sin, im_cos, im_sin = parts(sources[offset])
            weave(index, (re_cos + im_sin, im_cos - re_sin))

    @pl.when(side == 1)
    def _():
        row = lax.broadcasted_iota(jnp.int32, (LANES, LANES), 0)
        column = lax.broadcasted_iota(jnp.int32, (LANES, LANES), 1)
        mirror = (row + column == LANES - 1).astype(BF16)

        def mirrored(value):
            high = value.astype(BF16)
            middle, low = split(value - high.astype(F32))
            return dot_nn(high, mirror) + dot_nn(middle, mirror) + dot_nn(low, mirror)

        for index, offset in enumerate(offsets):
            re_cos, re_sin, im_cos, im_sin = parts(sources[offset])
            weave(index, (mirrored(re_cos - im_sin), mirrored(im_cos + re_sin)))

    def spectrum(offset):
        index = offsets.index(offset)
        return woven[index, 0], woven[index, 1]

    for out, slots, end in ((band_out, band_slots, 0), (partner_out, partner_slots, 1)):
        for place, own, gap in slots:
            keep = wanted[(end * planes + own) * band + gap] != 0
            own_re, own_im = spectrum(own)
            if end == 0:
                far_re, far_im = spectrum(own + gap)
                imag = own_im * far_re - own_re * far_im
            else:
                far_re, far_im = spectrum(own - gap)
                imag = far_re * own_im - far_im * own_re
            out[place + (0,)] = jnp.where(keep, own_re * far_re + own_im * far_im, 0.0)
            out[place + (1,)] = jnp.where(keep, imag, 0.0)


def cross(pairs, sources, earlier, planes, band, radix, last):
    share = radix * GROUP
    blocks = KX // 2 // LANES
    out = jax.ShapeDtypeStruct((planes, band, 2, share, KX), F32)

    def lane_block(block, side):
        return block + side * (2 * blocks - 1 - 2 * block)

    slots = {0: [], 1: []}
    if last:
        places = {0: (planes - 1, band - 1), 1: (0, band - 1)}
        slots = {0: [((0, 0), planes - 1, band - 1)], 1: [((0, 0), 0, band - 1)]}
        out_specs = tuple(
            pl.BlockSpec(
                (1, 1, 2, share, LANES),
                functools.partial(lambda end, b, side: places[end] + (0, 0, lane_block(b, side)), end),
            )
            for end in range(2)
        )
    else:
        for own in range(planes):
            for gap in range(band):
                for end in range(2):
                    far = own + gap if end == 0 else own - gap
                    if far in sources:
                        slots[end].append(((own, gap), own, gap))
        spec = pl.BlockSpec(
            (planes, band, 2, share, LANES), lambda b, side: (0, 0, 0, 0, lane_block(b, side))
        )
        out_specs = (spec, spec)
    used = sorted(
        {own for end in range(2) for _, own, _ in slots[end]}
        | {own + gap for _, own, gap in slots[0]}
        | {own - gap for _, own, gap in slots[1]}
    )
    specs = [pl.BlockSpec(memory_space=pltpu.SMEM)]
    specs += [pl.BlockSpec((1, 2 * share, 2 * LANES), lambda b, side: (0, 0, b))] * len(used)
    specs += [pl.BlockSpec(memory_space=pl.ANY)] * len(earlier)
    return pl.pallas_call(
        functools.partial(cross_kernel, radix, planes, used, slots[0], slots[1]),
        out_shape=(out, out),
        grid=(blocks, 2),
        in_specs=specs,
        out_specs=out_specs,
        scratch_shapes=[
            pltpu.SMEM((2 * planes * band,), jnp.int32),
            pltpu.VMEM((len(used), 2, share, LANES), F32),
        ],
        input_output_aliases={1 + len(used) + i: i for i in range(len(earlier))},
        compiler_params=pltpu.CompilerParams(vmem_limit_bytes=48 * 1024 * 1024),
        cost_estimate=pl.CostEstimate(
            flops=(len(slots[0]) + len(slots[1])) * share * KX * 6 + len(used) * share * KX * 200,
            bytes_accessed=(len(slots[0]) + len(slots[1]) + len(used)) * share * KX * 8,
            transcendentals=0,
        ),
        name="cross",
    )(pairs, *[sources[offset] for offset in used], *earlier)


def solution(mesh):
    shares = mesh.shape["pencil"]
    slabs = mesh.shape["plane"]
    reach = slabs // 2
    orders = halving_orders(shares)
    radix = KZ // shares // GROUP
    core_swap = [(i, i ^ 1) for i in range(shares)]
    swaps = [
        [(i, i ^ (1 << orders[i & 1][step])) for i in range(shares)] for step in range(len(orders[0]))
    ]
    upward = [(i, i + 1) for i in range(slabs - 1)]
    downward = [(i + 1, i) for i in range(slabs - 1)]

    def local(velocity, plane_slot, pair_list):
        planes, rows, nz = velocity.shape
        band = planes * reach
        whole, span, along_x = transform_calls(planes, rows, nz, shares, radix)

        def after(value, *earlier):
            return lax.optimization_barrier((value,) + earlier)[0]

        near, far = {}, {}
        first_hops, first_sum, last_sum = [], None, None
        for plane in range(planes):
            sent, kept = whole(plane, plane_slot, velocity)
            if plane:
                sent = after(sent, first_sum)
            terms = [kept, lax.ppermute(sent, "pencil", core_swap)]
            count = shares // 2
            for step, swap in enumerate(swaps):
                count //= 2
                leaving = functools.reduce(lambda a, b: a + b, [term[count : 2 * count] for term in terms])
                if plane and step == 1:
                    leaving = after(leaving, *first_hops)
                terms.append(lax.ppermute(leaving, "pencil", swap))
                if step == 0:
                    first_sum = terms[-1]
            last_sum = terms[-1]
            first_hops = []
            near[plane] = functools.reduce(lambda a, b: a + b, [term[:1] for term in terms])
            below, above = near[plane], near[plane]
            for away in range(1, reach + 1):
                home = near if away < reach else far
                if away < reach or plane > 0:
                    if away == reach and far:
                        below = after(below, *far.values())
                    below = lax.ppermute(below, "plane", upward)
                    home[plane - away * planes] = below
                    first_hops.append(below)
                if away < reach or plane < planes - 1:
                    above = lax.ppermute(above, "plane", downward)
                    home[plane + away * planes] = above
                    first_hops.append(above)
            first_hops = first_hops[:2]
        outputs = cross(pair_list, near, (), planes, band, radix, False)
        return tuple(cross(pair_list, {**near, **far}, outputs, planes, band, radix, True))

    return jax.shard_map(
        local,
        mesh=mesh,
        in_specs=(P("plane", "pencil", None), P(), P()),
        out_specs=(P("plane", None, None, "pencil", None), P("plane", None, None, "pencil", None)),
        check_vma=False,
    )
```

```python
import functools
import math

import ml_dtypes
import numpy as np

import jax
import jax.numpy as jnp
from jax import lax
from jax.experimental import pallas as pl
from jax.experimental.pallas import tpu as pltpu
from jax.sharding import PartitionSpec as P

KX = 512
KZ = 1024
LANES = 128
GROUP = 8
MIB = 1024 * 1024
F32 = jnp.float32
BF16 = jnp.bfloat16


def split_table(table):
    high = table.astype(np.float32).astype(ml_dtypes.bfloat16)
    low = (table - high.astype(np.float64)).astype(np.float32).astype(ml_dtypes.bfloat16)
    return high, low


def class_pairs(radix):
    return [(0, radix // 2)] + [(k, radix - k) for k in range(1, radix // 2)]


def span_table(nz, shares, radix):
    length = nz // radix
    padded = -(-length // LANES) * LANES
    per_owner = KZ // shares
    place = np.arange(length)
    pairs = []
    for number, pair in enumerate(class_pairs(radix)):
        table = np.zeros((2, shares, 2, GROUP, 2, padded))
        for member, residue in enumerate(pair):
            mode = np.arange(shares)[:, None] * per_owner + residue + radix * np.arange(GROUP)
            angle = (mode[..., None] * place % nz) * (2.0 * math.pi / nz)
            cosine, sine = np.cos(angle), np.sin(angle)
            if number == 0:
                table[0, :, member, :, member, :length] = cosine
                table[1, :, member, :, member, :length] = -sine
            else:
                sign = 1.0 if member == 0 else -1.0
                table[0, :, member, :, 0, :length] = cosine
                table[0, :, member, :, 1, :length] = sign * sine
                table[1, :, member, :, 0, :length] = -sine
                table[1, :, member, :, 1, :length] = sign * cosine
        pairs.append(table.reshape(2 * shares * 2 * GROUP, 2 * padded))
    high, low = split_table(np.stack(pairs))
    return np.concatenate([high, low], axis=1)


def axial_table(nx, nz, shares):
    pos = np.arange(nx).reshape(shares, nx // shares)
    column = np.arange(KX // 2)
    angle = ((2 * column + 1) * pos[..., None] % (2 * nx)) * (math.pi / nx)
    both = np.stack([np.cos(angle), np.sin(angle)], axis=2) / math.sqrt(nx * nz)
    both = both.reshape(shares, nx // shares, 2, -1, LANES).transpose(0, 1, 3, 2, 4)
    high, low = split_table(both.reshape(shares, nx // shares, KX))
    return np.concatenate([high, high, low], axis=1)


def shift_table(nx, shares):
    angle = np.arange(nx).reshape(shares, 1, nx // shares) * (math.pi / nx)
    rest = np.zeros((shares, 6, nx // shares))
    return np.concatenate([np.cos(angle), np.sin(angle), rest], axis=1).astype(np.float32)


def halving_orders(shares):
    bits = list(range(1, shares.bit_length() - 1))
    middle = len(bits) // 2
    return bits, bits[middle:] + bits[:middle]


def relative(index, order):
    top = len(order) - 1
    return sum(((index >> (top - step)) & 1) << bit for step, bit in enumerate(order))


def place_table(shares):
    orders = halving_orders(shares)
    rows = []
    for me in range(shares):
        other = me ^ 1
        sent = [other ^ relative(i, orders[other & 1]) for i in range(shares // 2)]
        kept = [me ^ relative(i, orders[me & 1]) for i in range(shares // 2)]
        rows.append(np.argsort(sent + kept))
    return np.array(rows, np.int32)


def split(value):
    high = value.astype(BF16)
    return high, (value - high.astype(F32)).astype(BF16)


def dot_nt(left, right):
    return lax.dot_general(left, right, (((1,), (1,)), ((), ())), preferred_element_type=F32)


def dot_nn(left, right):
    return lax.dot_general(left, right, (((1,), (0,)), ((), ())), preferred_element_type=F32)


def real_dft(values):
    count = len(values)
    if count == 1:
        return [(values[0], None)]
    if count == 2:
        return [(values[0] + values[1], None), (values[0] - values[1], None)]
    even = real_dft(values[0::2])
    odd = real_dft(values[1::2])
    out = [None] * (count // 2 + 1)
    for k in range(count // 4 + 1):
        even_re, even_im = even[k]
        odd_re, odd_im = odd[k]
        if k == 0:
            out[0] = (even_re + odd_re, None)
            out[count // 2] = (even_re - odd_re, None)
        elif 4 * k == count:
            out[k] = (even_re, -odd_re)
        else:
            cosine = math.cos(2.0 * math.pi * k / count)
            sine = math.sin(2.0 * math.pi * k / count)
            if 8 * k == count:
                turned_re = (odd_re + odd_im) * cosine
                turned_im = (odd_im - odd_re) * cosine
            else:
                turned_re = odd_re * cosine + odd_im * sine
                turned_im = odd_im * cosine - odd_re * sine
            out[k] = (even_re + turned_re, even_im + turned_im)
            out[count // 2 - k] = (even_re - turned_re, turned_im - even_im)
    return out


def fold_strip(radix, field, rows, fold_high, fold_low):
    nz = field.shape[1]
    length = nz // radix
    padded = -(-length // LANES) * LANES
    for piece in range(padded // LANES):
        blocks = []
        for block in range(radix):
            start = block * length + piece * LANES
            offset = start % LANES
            base = start - offset
            if offset == 0:
                blocks.append(field[rows, base : base + LANES])
            else:
                stop = min(base + 2 * LANES, nz)
                blocks.append(pltpu.roll(field[rows, base:stop], stop - base - offset, 1)[:, :LANES])
        waves = real_dft(blocks)
        for number, pair in enumerate(class_pairs(radix)):
            parts = (waves[0][0], waves[radix // 2][0]) if number == 0 else waves[pair[0]]
            for part in range(2):
                high, low = split(parts[part])
                columns = slice(part * padded + piece * LANES, part * padded + (piece + 1) * LANES)
                fold_high[number, rows, columns] = high
                fold_low[number, rows, columns] = low


def start_all(copies):
    for copy in copies:
        copy.start()


def span_phase(radix, plane, places, plane_slot, field, table, shift, y, scratch):
    velocity, span, turn, fold_high, fold_low, load_done, rest_done = scratch
    planes, rows, _ = field.shape
    shares = y.shape[0]
    me = lax.axis_index("pencil")
    first_plane = lax.axis_index("plane") * planes
    slot = plane_slot[first_plane + plane] - first_plane
    strip = 16
    cut = rows // load_done.shape[0]
    loads = []
    for piece in range(rows // cut):
        part = pl.ds(piece * cut, cut)
        loads.append(pltpu.make_async_copy(field.at[slot, part], velocity.at[part], load_done.at[piece]))
    rest = [
        pltpu.make_async_copy(table, span, rest_done.at[0]),
        pltpu.make_async_copy(shift.at[me], turn, rest_done.at[1]),
    ]
    start_all(loads)
    start_all(rest)
    yield
    for piece in range(rows // cut):
        loads[piece].wait()

        def fold(index, carry):
            first = pl.multiple_of(piece * cut + index * strip, strip)
            fold_strip(radix, velocity, pl.ds(first, strip), fold_high, fold_low)
            return carry

        lax.fori_loop(0, cut // strip, fold, 0, unroll=8 if cut % (8 * strip) == 0 else 2)
    for copy in rest:
        copy.wait()
    cos_shift = turn[0:1, :]
    sin_shift = turn[1:2, :]
    half = shares * 2 * GROUP
    for number in range(radix // 2):
        both = dot_nt(span[number], fold_high[number])
        value = both[: 2 * half] + both[2 * half :] + dot_nt(span[number, : 2 * half], fold_low[number])
        re_part = value[:half]
        im_part = value[half:]
        turned = (
            re_part * cos_shift - im_part * sin_shift,
            re_part * sin_shift + im_part * cos_shift,
        )
        for part in range(2):
            high, low = split(turned[part])
            first = (number * 2 + part) * 2 * GROUP
            for owner in range(shares):
                place = places[me * shares + owner]
                owned = slice(owner * 2 * GROUP, (owner + 1) * 2 * GROUP)
                y[place, first : first + 2 * GROUP, :rows] = high[owned]
                y[place, first : first + 2 * GROUP, rows:] = low[owned]
    yield


def axial_phase(y, wave, total, sent, kept, out_done):
    shares, count, width = y.shape
    half_count = shares // 2
    rows = width // 2
    owners = shares // out_done.shape[0]
    leaving = []
    for first in range(0, shares, owners):
        left = y[first : first + owners].reshape(owners * count, width)
        value = dot_nn(left, wave[:width]) + dot_nn(left[:, :rows], wave[width:])
        window = pl.ds(first, owners)
        total[window] = value.reshape(owners, count, KX)
        target = sent.at[window] if first < half_count else kept.at[pl.ds(first - half_count, owners)]
        leaving.append(pltpu.make_async_copy(total.at[window], target, out_done.at[first // owners]))
        leaving[-1].start()
    for copy in leaving:
        copy.wait()


def whole_kernel(radix, plane, places, plane_slot, field, table, shift, axial, sent, kept, y, wave, total, wave_done, out_done, *scratch):
    phase = span_phase(radix, plane, places, plane_slot, field, table, shift, y, scratch)
    next(phase)
    load = pltpu.make_async_copy(axial.at[lax.axis_index("pencil")], wave, wave_done)
    load.start()
    next(phase)
    load.wait()
    axial_phase(y, wave, total, sent, kept, out_done)


def transform_calls(planes, rows, nz, shares, radix):
    table = span_table(nz, shares, radix)
    axial = axial_table(rows * shares, nz, shares)
    shift = shift_table(rows * shares, shares)
    places = place_table(shares).reshape(-1)
    half_count = shares // 2
    pairs, table_rows, depth = table.shape
    count = pairs * 4 * GROUP
    owners = 2 if half_count % 2 == 0 else 1
    pieces = rows // LANES if rows % LANES == 0 else 1
    out = jax.ShapeDtypeStruct((half_count, count, KX), F32)
    modes = jax.ShapeDtypeStruct((shares, count, 2 * rows), BF16)
    smem = pl.BlockSpec(memory_space=pltpu.SMEM)
    hbm = pl.BlockSpec(memory_space=pltpu.HBM)
    free = pl.BlockSpec(memory_space=pl.ANY)
    one, many = pltpu.SemaphoreType.DMA(()), lambda number: pltpu.SemaphoreType.DMA((number,))
    y = pltpu.VMEM(modes.shape, BF16)
    span_scratch = [
        pltpu.VMEM((rows, nz), F32),
        pltpu.VMEM(table.shape, BF16),
        pltpu.VMEM(shift.shape[1:], F32),
        pltpu.VMEM((pairs, rows, depth), BF16),
        pltpu.VMEM((pairs, rows, depth), BF16),
        many(pieces),
        many(2),
    ]
    axial_scratch = [
        pltpu.VMEM(axial.shape[1:], BF16),
        pltpu.VMEM((shares, count, KX), F32),
        one,
        many(shares // owners),
    ]
    span_cost = (3 * rows * pairs * table_rows * depth, rows * nz * 4 + pairs * table_rows * depth * 2)
    axial_cost = (6 * shares * count * rows * KX, shares * count * (KX + rows) * 4)

    def call(kernel, name, limit, costs, ins, outs, scratch):
        return pl.pallas_call(
            kernel,
            out_shape=outs,
            in_specs=ins,
            out_specs=jax.tree.map(lambda _: free, outs),
            scratch_shapes=scratch,
            compiler_params=pltpu.CompilerParams(vmem_limit_bytes=limit),
            cost_estimate=pl.CostEstimate(
                flops=sum(cost[0] for cost in costs), bytes_accessed=sum(cost[1] for cost in costs), transcendentals=0
            ),
            name=name,
        )

    def whole(plane, plane_slot, field):
        return call(
            functools.partial(whole_kernel, radix, plane),
            "whole",
            40 * MIB if plane else 56 * MIB,
            [span_cost, axial_cost],
            [smem, smem, hbm, free if plane else hbm, hbm, hbm],
            (out, out),
            [y] + axial_scratch + span_scratch,
        )(places, plane_slot, field, table, shift, axial)

    return whole


def residues(radix):
    return [residue for pair in class_pairs(radix) for residue in pair]


def mirror_matrix():
    row = lax.broadcasted_iota(jnp.int32, (LANES, LANES), 0)
    column = lax.broadcasted_iota(jnp.int32, (LANES, LANES), 1)
    return (row + column == LANES - 1).astype(BF16)


def spectrum(radix, value, side, store):
    share = radix * GROUP
    value = value.reshape(radix // 2, 2, 2 * GROUP, 2 * LANES)
    re_rows = value[:, 0].reshape(share, 2 * LANES)
    im_rows = value[:, 1].reshape(share, 2 * LANES)
    re_cos, re_sin = re_rows[:, :LANES], re_rows[:, LANES:]
    im_cos, im_sin = im_rows[:, :LANES], im_rows[:, LANES:]
    if side == 0:
        parts = (re_cos + im_sin, im_cos - re_sin)
    else:
        mirror = mirror_matrix()

        def mirrored(part):
            high = part.astype(BF16)
            middle, low = split(part - high.astype(F32))
            return dot_nn(high, mirror) + dot_nn(middle, mirror) + dot_nn(low, mirror)

        parts = (mirrored(re_cos - im_sin), mirrored(im_cos + re_sin))
    for part in range(2):
        for number, residue in enumerate(residues(radix)):
            store(part, pl.ds(residue, GROUP, stride=radix), parts[part][number * GROUP : (number + 1) * GROUP])


def products(end, own, far):
    own_re, own_im = own
    far_re, far_im = far
    if end == 0:
        return own_re * far_re + own_im * far_im, own_im * far_re - own_re * far_im
    return far_re * own_re + far_im * own_im, far_re * own_im - far_im * own_re


def cross_kernel(radix, planes, offsets, slots, pairs, *refs):
    sources = dict(zip(offsets, refs[: len(offsets)]))
    outs, wanted, woven = refs[-4:-2], refs[-2], refs[-1]
    band = wanted.shape[0] // (2 * planes)
    side = pl.program_id(1)

    @pl.when((pl.program_id(0) == 0) & (side == 0))
    def _():
        first_plane = lax.axis_index("plane") * planes

        def clear(index, carry):
            wanted[index] = 0
            return carry

        lax.fori_loop(0, 2 * planes * band, clear, 0)

        def mark(index, carry):
            lower = pairs[index, 0]
            upper = pairs[index, 1]
            for end, plane in enumerate((lower - first_plane, upper - first_plane)):

                @pl.when((plane >= 0) & (plane < planes))
                def _():
                    wanted[(end * planes + plane) * band + upper - lower] = 1

            return carry

        lax.fori_loop(0, pairs.shape[0], mark, 0)

    def weave(index, part, rows, value):
        woven[index, part, rows, :] = value

    for value in range(2):

        @pl.when(side == value)
        def _():
            for index, offset in enumerate(offsets):
                spectrum(radix, sources[offset][0], value, functools.partial(weave, index))

    def woven_parts(offset):
        index = offsets.index(offset)
        return woven[index, 0], woven[index, 1]

    for end, own, gap in slots:
        keep = wanted[(end * planes + own) * band + gap] != 0
        far = own + gap if end == 0 else own - gap
        for part, value in enumerate(products(end, woven_parts(own), woven_parts(far))):
            outs[end][own, gap, part] = jnp.where(keep, value, 0.0)


def cross(pairs, near, planes, band, radix):
    share = radix * GROUP
    blocks = KX // 2 // LANES
    slots = [
        (end, own, gap)
        for own in range(planes)
        for gap in range(band)
        for end in range(2)
        if (own + gap if end == 0 else own - gap) in near
    ]
    offsets = sorted(near)
    out = jax.ShapeDtypeStruct((planes, band, 2, share, KX), F32)
    spec = pl.BlockSpec(
        (planes, band, 2, share, LANES), lambda b, side: (0, 0, 0, 0, b + side * (2 * blocks - 1 - 2 * b))
    )
    smem = pl.BlockSpec(memory_space=pltpu.SMEM)
    return pl.pallas_call(
        functools.partial(cross_kernel, radix, planes, offsets, slots),
        out_shape=(out, out, jax.ShapeDtypeStruct((2 * planes * band,), jnp.int32)),
        grid=(blocks, 2),
        in_specs=[smem] + [pl.BlockSpec((1, 2 * share, 2 * LANES), lambda b, side: (0, 0, b))] * len(offsets),
        out_specs=(spec, spec, smem),
        scratch_shapes=[pltpu.VMEM((len(offsets), 2, share, LANES), F32)],
        compiler_params=pltpu.CompilerParams(vmem_limit_bytes=32 * MIB),
        cost_estimate=pl.CostEstimate(
            flops=len(slots) * share * KX * 6 + len(offsets) * share * KX * 200,
            bytes_accessed=(len(slots) + len(offsets)) * share * KX * 8,
            transcendentals=0,
        ),
        name="cross",
    )(pairs, *[near[offset] for offset in offsets])


def cross_last_kernel(radix, planes, band, wanted, *refs):
    sources, outs, woven = refs[:4], refs[-3:-1], refs[-1]
    blocks = KX // 2 // LANES
    for end in range(2):
        own = planes - 1 if end == 0 else 0
        keep = wanted[(end * planes + own) * band + band - 1] != 0
        for block in range(blocks):
            for side in range(2):
                place = block if side == 0 else 2 * blocks - 1 - block
                lanes = slice(place * LANES, (place + 1) * LANES)
                columns = slice(block * 2 * LANES, (block + 1) * 2 * LANES)
                for index in range(2):

                    def weave(part, rows, value):
                        woven[end, place, index, part, rows, :] = value

                    spectrum(radix, sources[2 * end + index][0, :, columns], side, weave)
                spectra = [(woven[end, place, index, 0], woven[end, place, index, 1]) for index in range(2)]
                for part, value in enumerate(products(end, *spectra)):
                    outs[end][0, 0, part, :, lanes] = jnp.where(keep, value, 0.0)


def cross_last(wanted, sources, earlier, planes, band, radix):
    share = radix * GROUP
    out = jax.ShapeDtypeStruct((planes, band, 2, share, KX), F32)
    whole = pl.BlockSpec((1, 2 * share, KX), lambda i: (0, 0, 0))
    places = ((planes - 1, band - 1), (0, band - 1))
    return pl.pallas_call(
        functools.partial(cross_last_kernel, radix, planes, band),
        out_shape=(out, out),
        grid=(1,),
        in_specs=[pl.BlockSpec(memory_space=pltpu.SMEM)] + [whole] * 4 + [pl.BlockSpec(memory_space=pl.ANY)] * 2,
        out_specs=tuple(
            pl.BlockSpec((1, 1, 2, share, KX), functools.partial(lambda place, i: place + (0, 0, 0), place))
            for place in places
        ),
        scratch_shapes=[pltpu.VMEM((2, KX // LANES, 2, 2, share, LANES), F32)],
        input_output_aliases={5: 0, 6: 1},
        compiler_params=pltpu.CompilerParams(vmem_limit_bytes=32 * MIB),
        cost_estimate=pl.CostEstimate(
            flops=share * KX * 900, bytes_accessed=8 * share * KX * 8, transcendentals=0
        ),
        name="cross_last",
    )(wanted, *sources, *earlier)


def solution(mesh):
    shares = mesh.shape["pencil"]
    slabs = mesh.shape["plane"]
    reach = slabs // 2
    orders = halving_orders(shares)
    radix = KZ // shares // GROUP
    core_swap = [(i, i ^ 1) for i in range(shares)]
    swaps = [
        [(i, i ^ (1 << orders[i & 1][step])) for i in range(shares)] for step in range(len(orders[0]))
    ]
    upward = [(i, i + 1) for i in range(slabs - 1)]
    downward = [(i + 1, i) for i in range(slabs - 1)]

    def local(velocity, plane_slot, pair_list):
        planes, rows, nz = velocity.shape
        band = planes * reach
        whole = transform_calls(planes, rows, nz, shares, radix)

        def after(value, *earlier):
            return lax.optimization_barrier((value,) + earlier)[0]

        near, far = {}, {}
        first_hops, first_sum, last_sum = [], None, None
        for plane in range(planes):
            sent, kept = whole(plane, plane_slot, velocity)
            if plane:
                sent = after(sent, first_sum)
            terms = [kept, lax.ppermute(sent, "pencil", core_swap)]
            count = shares // 2
            for step, swap in enumerate(swaps):
                count //= 2
                leaving = functools.reduce(lambda a, b: a + b, [term[count : 2 * count] for term in terms])
                if plane and step == 1:
                    leaving = after(leaving, *first_hops)
                terms.append(lax.ppermute(leaving, "pencil", swap))
                if step == 0:
                    first_sum = terms[-1]
            last_sum = terms[-1]
            first_hops = []
            near[plane] = functools.reduce(lambda a, b: a + b, [term[:1] for term in terms])
            below, above = near[plane], near[plane]
            for away in range(1, reach + 1):
                home = near if away < reach else far
                if away < reach or plane > 0:
                    if away == reach and far:
                        below = after(below, *far.values())
                    below = lax.ppermute(below, "plane", upward)
                    home[plane - away * planes] = below
                    first_hops.append(below)
                if away < reach or plane < planes - 1:
                    above = lax.ppermute(above, "plane", downward)
                    home[plane + away * planes] = above
                    first_hops.append(above)
            first_hops = first_hops[:2]
        *outputs, wanted = cross(pair_list, near, planes, band, radix)
        sources = [near[planes - 1], far[planes - 1 + band - 1], near[0], far[1 - band]]
        return tuple(cross_last(wanted, sources, outputs, planes, band, radix))

    return jax.shard_map(
        local,
        mesh=mesh,
        in_specs=(P("plane", "pencil", None), P(), P()),
        out_specs=(P("plane", None, None, "pencil", None), P("plane", None, None, "pencil", None)),
        check_vma=False,
    )
```
